32 devices in a mesh: sect: 2 (over x), wide: 4 (over y, core), narrow: 4 (over z).
Axes of the slice: x: 2, y: 2, z: 4, core: 2. Of those that a mesh axis runs over, the one named last changes fastest.
Arguments:
- leaf_rhs: bfloat16 [512, 8192], P('wide', ('sect', 'narrow')), may hold values from -6 to 6
- leaf_factor: bfloat16 [8192, 4096], P(('sect', 'wide'), 'narrow'), may hold values from -1 to 2
- leaf_coupling: bfloat16 [4096, 4096], P(('sect', 'wide'), 'narrow'), may hold values from -0.09375 to 0.09375
- root_factor: bfloat16 [16384, 16384], P('wide', ('sect', 'narrow')), may hold values from -1 to 2
- root_rhs: bfloat16 [512, 16384], P('wide', ('sect', 'narrow')), may hold values from -6 to 6
- border_map: int32 [2, 2048], replicated, may hold values from 0 to 16383, as said below
- border_rows: int32 [2], replicated, may hold values from 512 to 2048, as said below
Outputs:
- leaf_solution: bfloat16 [512, 8192], P('wide', ('sect', 'narrow'))
- root_solution: bfloat16 [512, 16384], P('wide', ('sect', 'narrow'))
The draws below stay inside these ranges and needn't reach their ends.
Inputs may be any that keep to these rules, and one draw needn't show every extreme that they name: `border_map`: row s lists the root indices of the 2048 border rows of leaf s, all different within a row; different leaves may share root indices. The live border rows of leaf s are its first border_rows[s] rows.
All inputs are finite; a program needn't handle non-finite values.
Results may differ from the reference program's by a relative error of at most 0.024.
Values may be sent and summed in bfloat16 or wider, within the bound.
No kernel may reach another device: no remote copies, remote signals or barrier semaphores. Data moves between devices by JAX's collectives and lax.ppermute only.
A program may use at most 64 MiB of HBM per device.

```python
import math
import jax
import jax.numpy as jnp
from jax import lax

RHS = 512
PIVOTS = 4096
BORDER = 2048
ROOT = 16384
LEAVES = 2
LEAF_SPLIT = 4
ROOT_SPLIT = 8
ROW_SPLIT = 4


def factor_draw(key, rows, columns):
    spread_key, diagonal_key = jax.random.split(key)
    spread = jnp.clip(jax.random.normal(spread_key, (rows, columns), jnp.float32), -5.0, 5.0) * (0.4 / math.sqrt(columns))
    diagonal = jax.random.uniform(diagonal_key, (rows, 1), jnp.float32, 0.6, 1.4)
    row_place = lax.broadcasted_iota(jnp.int32, (rows, columns), 0) % columns
    column_place = lax.broadcasted_iota(jnp.int32, (rows, columns), 1)
    return (spread + jnp.where(row_place == column_place, diagonal, 0.0)).astype(jnp.bfloat16)


def draw_leaf_factor(key, part):
    return factor_draw(jax.random.fold_in(key, 11), LEAVES * PIVOTS, PIVOTS)


def draw_root_factor(key, part):
    return factor_draw(jax.random.fold_in(key, 13), ROOT, ROOT)


def draw_border_map(key, part):
    leaf_keys = jax.random.split(jax.random.fold_in(key, 17), LEAVES)

    def one_leaf(leaf_key):
        order = jax.random.permutation(leaf_key, ROOT).astype(jnp.int32)
        order = (order + (ROOT - 1 - order[0])) % ROOT
        return order[:BORDER]
    return jax.vmap(one_leaf)(leaf_keys).astype(jnp.int32)


def draw_border_rows(key, part):
    count_key, full_key = jax.random.split(jax.random.fold_in(key, 19))
    counts = jax.random.randint(count_key, (LEAVES,), BORDER // 4, BORDER + 1, jnp.int32)
    chosen = jax.random.randint(full_key, (), 0, LEAVES, jnp.int32)
    places = lax.broadcasted_iota(jnp.int32, (LEAVES,), 0)
    return jnp.where(places == chosen, BORDER, counts).astype(jnp.int32)


def levels(own_key, shape, cuts, least, largest):
    def one(dim, shards_of):
        heights = jax.random.uniform(jax.random.fold_in(jax.random.fold_in(own_key, 6), dim), (shards_of,), jnp.float32, least / len(cuts), largest / len(cuts))
        return jnp.repeat(jnp.exp(heights), shape[dim] // shards_of).reshape((-1,) + (1,) * (len(shape) - dim - 1))

    factor_of = one(*cuts[0])
    for cut in cuts[1:]:
        factor_of = factor_of * one(*cut)
    return factor_of


def bell_draw(stream_key, shape, deviation, reach, cuts=(), kind=jnp.bfloat16):
    array = jax.random.normal(stream_key, shape, jnp.float32) * deviation
    if len(cuts) > 0:
        array = levels(stream_key, shape, cuts, -0.22, 0.18) * array
    return jnp.clip(array, min=-reach, max=reach).astype(kind)


def setup_inputs(seed: int = 0) -> dict:
    streams_of = jax.random.split(jax.random.key(seed), 8)
    return {
        "leaf_rhs": bell_draw(streams_of[0], (RHS, LEAVES * PIVOTS), 1.0, 6.0, ((0, 4), (1, 8))),
        "leaf_factor": draw_leaf_factor(jax.random.fold_in(streams_of[7], 71), 0),
        "leaf_coupling": bell_draw(streams_of[2], (LEAVES * BORDER, PIVOTS), PIVOTS ** -0.5, 0.09375, ((0, 8), (1, 4))),
        "root_factor": draw_root_factor(jax.random.fold_in(streams_of[7], 71), 0),
        "root_rhs": bell_draw(streams_of[4], (RHS, ROOT), 1.0, 6.0, ((0, 4), (1, 8))),
        "border_map": draw_border_map(jax.random.fold_in(streams_of[7], 71), 0),
        "border_rows": draw_border_rows(jax.random.fold_in(streams_of[7], 71), 0),
    }


def rounded(value):
    return lax.optimization_barrier(value.astype(jnp.bfloat16)).astype(jnp.float32)


def times_transposed(left, right):
    return lax.dot_general(left, right, (((1,), (1,)), ((), ())), preferred_element_type=jnp.float32)


def reference(leaf_rhs, leaf_factor, leaf_coupling, root_factor, root_rhs, border_map, border_rows):
    column_width = PIVOTS // LEAF_SPLIT
    border_place = lax.broadcasted_iota(jnp.int32, (1, BORDER), 1)
    leaf_mids = []
    border_parts = []
    for leaf_index in range(LEAVES):
        rhs_leaf = leaf_rhs[:, leaf_index * PIVOTS:(leaf_index + 1) * PIVOTS]
        factor = leaf_factor[leaf_index * PIVOTS:(leaf_index + 1) * PIVOTS]
        coupling = leaf_coupling[leaf_index * BORDER:(leaf_index + 1) * BORDER]
        stacked = jnp.concatenate([factor, coupling], axis=0)
        summed = jnp.zeros((RHS, PIVOTS + BORDER), jnp.float32)
        for block in range(LEAF_SPLIT):
            columns = slice(block * column_width, (block + 1) * column_width)
            summed = summed + rounded(times_transposed(rhs_leaf[:, columns], stacked[:, columns]))
        leaf_mids.append(summed[:, :PIVOTS].astype(jnp.bfloat16))
        active = border_place < border_rows[leaf_index]
        border_parts.append(jnp.where(active, summed[:, PIVOTS:], jnp.float32(0.0)).astype(jnp.bfloat16))
    extend = jnp.zeros((RHS, ROOT), jnp.float32)
    for leaf_index in range(LEAVES):
        extend = extend.at[:, border_map[leaf_index]].add(border_parts[leaf_index].astype(jnp.float32))
    root_right = (root_rhs.astype(jnp.float32) - extend).astype(jnp.bfloat16)

    root_width = ROOT // ROOT_SPLIT

    def forward_block(block, summed):
        right_columns = lax.dynamic_slice_in_dim(root_right, block * root_width, root_width, 1)
        factor_columns = lax.dynamic_slice_in_dim(root_factor, block * root_width, root_width, 1)
        return summed + rounded(times_transposed(right_columns, factor_columns))

    root_mid = lax.fori_loop(0, ROOT_SPLIT, forward_block, jnp.zeros((RHS, ROOT), jnp.float32)).astype(jnp.bfloat16)

    row_width = ROOT // ROW_SPLIT

    def back_block(block, summed):
        mid_columns = lax.dynamic_slice_in_dim(root_mid, block * row_width, row_width, 1)
        factor_rows = lax.dynamic_slice_in_dim(root_factor, block * row_width, row_width, 0)
        return summed + rounded(jnp.dot(mid_columns, factor_rows, preferred_element_type=jnp.float32))

    root_solution = lax.fori_loop(0, ROW_SPLIT, back_block, jnp.zeros((RHS, ROOT), jnp.float32)).astype(jnp.bfloat16)

    pivot_width = PIVOTS // ROW_SPLIT
    border_width = BORDER // ROW_SPLIT
    solutions = []
    for leaf_index in range(LEAVES):
        factor = leaf_factor[leaf_index * PIVOTS:(leaf_index + 1) * PIVOTS]
        coupling = leaf_coupling[leaf_index * BORDER:(leaf_index + 1) * BORDER]
        active = border_place < border_rows[leaf_index]
        returned = jnp.where(active, root_solution[:, border_map[leaf_index]], jnp.zeros((), jnp.bfloat16))
        summed = jnp.zeros((RHS, PIVOTS), jnp.float32)
        for block in range(ROW_SPLIT):
            pivot_span = slice(block * pivot_width, (block + 1) * pivot_width)
            border_span = slice(block * border_width, (block + 1) * border_width)
            difference = jnp.dot(leaf_mids[leaf_index][:, pivot_span], factor[pivot_span], preferred_element_type=jnp.float32)
            difference = difference - jnp.dot(returned[:, border_span], coupling[border_span], preferred_element_type=jnp.float32)
            summed = summed + rounded(difference)
        solutions.append(summed.astype(jnp.bfloat16))
    leaf_solution = jnp.concatenate(solutions, axis=1)
    return leaf_solution, root_solution
```

```python
import jax
import jax.numpy as jnp
from jax import lax
from jax.sharding import PartitionSpec as P

CHUNKS = 4


def times_transposed(left, right):
    return lax.dot_general(
        left, right, (((1,), (1,)), ((), ())), preferred_element_type=jnp.float32
    )


def times(left, right):
    return jnp.dot(left, right, preferred_element_type=jnp.float32)


def tie(values, others):
    return lax.optimization_barrier(tuple(values) + tuple(others))[: len(values)]


def swap(value, axis, distance):
    pairs = [(i, i ^ distance) for i in range(lax.axis_size(axis))]
    return lax.ppermute(value, axis, pairs)


def total(values):
    result = values[0].astype(jnp.float32)
    for value in values[1:]:
        result = result + value.astype(jnp.float32)
    return result.astype(jnp.bfloat16)


def relative_gather(value, axis):
    distance = lax.axis_size(axis) // 2
    while distance >= 1:
        value = jnp.concatenate([value, swap(value, axis, distance)], axis=0)
        distance //= 2
    return value


def relative_scatter(value, axis):
    distance = 1
    while distance < lax.axis_size(axis):
        half = value.shape[0] // 2
        value = total([value[:half], swap(value[half:].astype(jnp.bfloat16), axis, distance)])
        distance *= 2
    return value


def relative_places(axis):
    places = [0]
    distance = lax.axis_size(axis) // 2
    while distance >= 1:
        places = places + [place ^ distance for place in places]
        distance //= 2
    return places


def direct_scatter(value, axis, dim=0):
    count = lax.axis_size(axis)
    here = lax.axis_index(axis)
    block = value.shape[dim] // count
    shape = value.shape[:dim] + (count, block) + value.shape[dim + 1 :]
    blocks = value.reshape(shape)
    parts = [lax.dynamic_index_in_dim(blocks, here ^ k, dim, keepdims=False) for k in range(count)]
    return total([parts[0]] + [swap(parts[k], axis, k) for k in range(1, count)])


def direct_gather(value, axis, dim=0):
    count = lax.axis_size(axis)
    here = lax.axis_index(axis)
    shape = value.shape[:dim] + (count,) + value.shape[dim:]
    result = jnp.zeros(shape, value.dtype)
    for k in range(count):
        block = value if k == 0 else swap(value, axis, k)
        result = lax.dynamic_update_index_in_dim(result, block, here ^ k, dim)
    return result.reshape(value.shape[:dim] + (count * value.shape[dim],) + value.shape[dim + 1 :])


def root_solve(right, factor):
    rows = factor.shape[0] // CHUNKS
    blocks = [factor[c * rows : (c + 1) * rows] for c in range(CHUNKS)]
    value = {("product", c): times_transposed(right, blocks[c]).astype(jnp.bfloat16) for c in range(CHUNKS)}
    steps = {
        "sect_sum": (lambda v: direct_scatter(v, "sect"), "product"),
        "narrow_sum": (lambda v: direct_scatter(v, "narrow"), "sect_sum"),
        "narrow_all": (lambda v: direct_gather(v, "narrow"), "narrow_sum"),
        "sect_all": (lambda v: direct_gather(v, "sect"), "narrow_all"),
    }
    rounds = [
        [("sect_sum", 0)],
        [("narrow_sum", 0), ("sect_sum", 1)],
        [("narrow_all", 0), ("sect_sum", 2)],
        [("narrow_sum", 1), ("sect_all", 0)],
        [("narrow_all", 1), ("sect_sum", 3)],
        [("narrow_sum", 2), ("sect_all", 1)],
        [("narrow_all", 2)],
        [("narrow_sum", 3), ("sect_all", 2)],
        [("narrow_all", 3)],
        [("sect_all", 3)],
    ]
    before = []
    for turn in rounds:
        taken = [value[(steps[name][1], c)] for name, c in turn]
        if before:
            taken = tie(taken, before)
        before = [steps[name][0](v) for (name, c), v in zip(turn, taken)]
        for key, v in zip(turn, before):
            value[key] = v
    back = None
    for c in range(CHUNKS):
        term = times(value[("sect_all", c)], blocks[c])
        back = term if back is None else back + term
    return back, value[("narrow_all", CHUNKS - 1)]


def body(leaf_rhs, leaf_factor, leaf_coupling, root_factor, root_rhs, border_map, border_rows):
    wide_count = lax.axis_size("wide")
    narrow_count = lax.axis_size("narrow")
    sect_count = lax.axis_size("sect")
    sect_index = lax.axis_index("sect")
    wide_index = lax.axis_index("wide")
    narrow_index = lax.axis_index("narrow")
    border_block = leaf_coupling.shape[0]
    border_total = border_block * wide_count
    rows = leaf_rhs.shape[0]
    small = rows // narrow_count
    root_block = root_rhs.shape[1]
    root_start = (sect_index * narrow_count + narrow_index) * root_block

    columns = lax.broadcasted_iota(jnp.int32, (1, 1, root_block), 2) + root_start
    border_place = lax.broadcasted_iota(jnp.int32, border_map.shape, 1)
    live_map = jnp.where(border_place < border_rows[:, None], border_map, -1)
    landing = (live_map[:, :, None] == columns).astype(jnp.bfloat16)

    piece = relative_gather(leaf_rhs, "wide")
    places = relative_places("wide")
    border_terms = times_transposed(piece, leaf_coupling).astype(jnp.bfloat16)
    blocks = border_terms.reshape(wide_count, rows, border_block)
    order = [places.index(k) for k in range(wide_count)]

    def by_place(values, dim=0):
        near = [lax.index_in_dim(values, order[k], dim, keepdims=False) for k in range(wide_count)]
        near = jnp.stack(near, axis=dim)
        return jnp.stack(
            [lax.dynamic_index_in_dim(near, wide_index ^ k, dim, keepdims=False) for k in range(wide_count)],
            axis=dim,
        )

    def by_relation(values, dim=0):
        return jnp.stack(
            [lax.dynamic_index_in_dim(values, wide_index ^ p, dim, keepdims=False) for p in places],
            axis=dim,
        )

    sent = by_place(blocks).reshape(wide_count * narrow_count, small, border_block)
    got = lax.all_to_all(sent, ("wide", "narrow"), 0, 0, tiled=True)
    border_sum = jnp.sum(
        got.reshape(wide_count, narrow_count, small, border_block).astype(jnp.float32), axis=1
    )
    border_out = border_sum.transpose(1, 0, 2).reshape(small, border_total).astype(jnp.bfloat16)

    updates = direct_gather(border_out, "narrow")
    updates = direct_gather(updates[None], "sect")
    landed = jnp.zeros((rows, root_block), jnp.float32)
    for s in range(sect_count):
        landed = landed + times(updates[s], landing[s])
    root_right = (root_rhs.astype(jnp.float32) - landed).astype(jnp.bfloat16)
    right = relative_gather(root_right, "wide")

    (piece_late,) = tie([piece], [updates])
    pivot_terms = times_transposed(piece_late, leaf_factor).astype(jnp.bfloat16)
    pivot_terms = pivot_terms.reshape(wide_count, rows, -1)
    leaf_mid = lax.psum_scatter(pivot_terms, "narrow", scatter_dimension=1, tiled=True)

    back, late = root_solve(right, root_factor)
    root_solution = relative_scatter(back, "wide")

    (leaf_mid,) = tie([leaf_mid], [late])
    leaf_mid = lax.all_gather(leaf_mid, "narrow", axis=1, tiled=True).reshape(wide_count * rows, -1)

    picked = [
        times_transposed(root_solution, landing[s]).astype(jnp.bfloat16) for s in range(sect_count)
    ]
    picked = jnp.stack(picked).reshape(sect_count, narrow_count, small, wide_count, border_block)
    sent = picked.transpose(0, 3, 1, 2, 4).reshape(-1, small, border_block)
    got = lax.all_to_all(sent, ("sect", "wide", "narrow"), 0, 0, tiled=True)
    got = got.reshape(sect_count, wide_count, narrow_count, small, border_block)
    own = jnp.sum(got.astype(jnp.float32), axis=(0, 2)).astype(jnp.bfloat16)
    returned = direct_gather(by_relation(own), "narrow", 1).reshape(wide_count * rows, border_block)

    back_leaf = times(leaf_mid, leaf_factor) - times(returned, leaf_coupling)
    leaf_solution = relative_scatter(back_leaf, "wide")
    return (leaf_solution, root_solution)


def solution(mesh):
    in_specs = (
        P("wide", ("sect", "narrow")),
        P(("sect", "wide"), "narrow"),
        P(("sect", "wide"), "narrow"),
        P("wide", ("sect", "narrow")),
        P("wide", ("sect", "narrow")),
        P(),
        P(),
    )
    out_specs = (P("wide", ("sect", "narrow")), P("wide", ("sect", "narrow")))
    return jax.shard_map(body, mesh=mesh, in_specs=in_specs, out_specs=out_specs, check_vma=False)
```

```python
import jax
import jax.numpy as jnp
from jax import lax
from jax.sharding import PartitionSpec as P

CHUNKS = 4


def times_transposed(left, right):
    return lax.dot_general(
        left, right, (((1,), (1,)), ((), ())), preferred_element_type=jnp.float32
    )


def times(left, right):
    return jnp.dot(left, right, preferred_element_type=jnp.float32)


def hold(value, other):
    corner = lax.slice(other, (0,) * other.ndim, (1,) * other.ndim).reshape(())
    zero = lax.clamp(jnp.int32(0), corner.astype(jnp.int32), jnp.int32(0))
    return value + zero.astype(value.dtype)


def swap(value, axis, distance):
    pairs = [(i, i ^ distance) for i in range(lax.axis_size(axis))]
    return lax.ppermute(value, axis, pairs)


def total(values):
    result = values[0].astype(jnp.float32)
    for value in values[1:]:
        result = result + value.astype(jnp.float32)
    return result.astype(jnp.bfloat16)


def relative_gather(value, axis, last=1):
    distance = lax.axis_size(axis) // 2
    while distance >= last:
        value = jnp.concatenate([value, swap(value, axis, distance)], axis=0)
        distance //= 2
    return value


def relative_scatter(value, axis, distance=1):
    while distance < lax.axis_size(axis):
        half = value.shape[0] // 2
        value = total([value[:half], swap(value[half:].astype(jnp.bfloat16), axis, distance)])
        distance *= 2
    return value


def relative_places(axis):
    places = [0]
    distance = lax.axis_size(axis) // 2
    while distance >= 1:
        places = places + [place ^ distance for place in places]
        distance //= 2
    return places


def direct_scatter(value, axis, dim=0):
    count = lax.axis_size(axis)
    here = lax.axis_index(axis)
    block = value.shape[dim] // count
    shape = value.shape[:dim] + (count, block) + value.shape[dim + 1 :]
    blocks = value.reshape(shape)
    parts = [lax.dynamic_index_in_dim(blocks, here ^ k, dim, keepdims=False) for k in range(count)]
    return total([parts[0]] + [swap(parts[k], axis, k) for k in range(1, count)])


def direct_gather(value, axis, dim=0):
    count = lax.axis_size(axis)
    here = lax.axis_index(axis)
    shape = value.shape[:dim] + (count,) + value.shape[dim:]
    result = jnp.zeros(shape, value.dtype)
    for k in range(count):
        block = value if k == 0 else swap(value, axis, k)
        result = lax.dynamic_update_index_in_dim(result, block, here ^ k, dim)
    return result.reshape(value.shape[:dim] + (count * value.shape[dim],) + value.shape[dim + 1 :])


def halve(value, axis, distance, other=None):
    bit = (lax.axis_index(axis) // distance) % 2
    halves = value.reshape((2, value.shape[0] // 2) + value.shape[1:])
    kept, given = (lax.dynamic_index_in_dim(halves, k, 0, keepdims=False) for k in (bit, 1 - bit))
    if other is not None:
        given = hold(given, other)
    return total([kept, swap(given, axis, distance)])


def double(value, axis, distance):
    bit = (lax.axis_index(axis) // distance) % 2
    result = jnp.zeros((2,) + value.shape, value.dtype)
    result = lax.dynamic_update_index_in_dim(result, value, bit, 0)
    result = lax.dynamic_update_index_in_dim(result, swap(value, axis, distance), 1 - bit, 0)
    return result.reshape((2 * value.shape[0],) + value.shape[1:])


def distances(axis):
    return [(axis, 1 << k) for k in range(lax.axis_size(axis).bit_length() - 1)]


def sum_all(value, order, other):
    first = value = halve(value, *order[0], other)
    for axis, distance in order[1:]:
        value = halve(value, axis, distance)
    for axis, distance in reversed(order):
        value = double(value, axis, distance)
    return value, first


def root_solve(right, factor, beside):
    rows = factor.shape[0] // CHUNKS
    half = right.shape[0] // 2
    sect, narrow = distances("sect"), distances("narrow")
    orders = [sect + narrow, narrow[:1] + sect + narrow[1:]]
    blocks = [factor[c * rows : (c + 1) * rows] for c in range(CHUNKS)]
    middles, firsts = [], []
    for c in range(CHUNKS):
        product = times_transposed(right, blocks[c]).astype(jnp.bfloat16)
        other = firsts[c - len(orders)] if c >= len(orders) else beside
        middle, first = sum_all(product, orders[c % len(orders)], other)
        middles.append(middle)
        firsts.append(first)
    backs = []
    for part in (slice(half, None), slice(0, half)):
        back = None
        for c in range(CHUNKS):
            term = times(middles[c][part], blocks[c])
            back = term if back is None else back + term
        backs.append(back)
    return backs, middles


def body(leaf_rhs, leaf_factor, leaf_coupling, root_factor, root_rhs, border_map, border_rows):
    wide_count = lax.axis_size("wide")
    narrow_count = lax.axis_size("narrow")
    sect_count = lax.axis_size("sect")
    sect_index = lax.axis_index("sect")
    wide_index = lax.axis_index("wide")
    narrow_index = lax.axis_index("narrow")
    border_block = leaf_coupling.shape[0]
    border_total = border_block * wide_count
    rows = leaf_rhs.shape[0]
    small = rows // narrow_count
    root_block = root_rhs.shape[1]
    root_start = (sect_index * narrow_count + narrow_index) * root_block

    columns = lax.broadcasted_iota(jnp.int32, (1, 1, root_block), 2) + root_start
    border_place = lax.broadcasted_iota(jnp.int32, border_map.shape, 1)
    live_map = jnp.where(border_place < border_rows[:, None], border_map, -1)
    landing = (live_map[:, :, None] == columns).astype(jnp.bfloat16)

    piece = relative_gather(leaf_rhs, "wide")
    places = relative_places("wide")
    border_terms = times_transposed(piece, leaf_coupling).astype(jnp.bfloat16)
    blocks = border_terms.reshape(wide_count, rows, border_block)
    order = [places.index(k) for k in range(wide_count)]

    def by_place(values, dim=0):
        near = [lax.index_in_dim(values, order[k], dim, keepdims=False) for k in range(wide_count)]
        near = jnp.stack(near, axis=dim)
        return jnp.stack(
            [lax.dynamic_index_in_dim(near, wide_index ^ k, dim, keepdims=False) for k in range(wide_count)],
            axis=dim,
        )

    def by_relation(values, dim=0):
        return jnp.stack(
            [lax.dynamic_index_in_dim(values, wide_index ^ p, dim, keepdims=False) for p in places],
            axis=dim,
        )

    sent = by_place(blocks).reshape(wide_count * narrow_count, small, border_block)
    got = lax.all_to_all(sent, ("wide", "narrow"), 0, 0, tiled=True)
    border_sum = jnp.sum(
        got.reshape(wide_count, narrow_count, small, border_block).astype(jnp.float32), axis=1
    )
    border_out = border_sum.transpose(1, 0, 2).reshape(small, border_total).astype(jnp.bfloat16)

    updates = direct_gather(border_out, "narrow")
    pivot_terms = times_transposed(piece, leaf_factor).astype(jnp.bfloat16)
    pivot_terms = hold(pivot_terms.reshape(wide_count, rows, -1), updates)
    leaf_mid = lax.psum_scatter(pivot_terms, "narrow", scatter_dimension=1, tiled=True)
    updates = direct_gather(updates[None], "sect")
    landed = jnp.zeros((rows, root_block), jnp.float32)
    for s in range(sect_count):
        landed = landed + times(updates[s], landing[s])
    root_right = (root_rhs.astype(jnp.float32) - landed).astype(jnp.bfloat16)
    right = relative_gather(root_right, "wide", 2)
    right = jnp.concatenate([right, swap(right, "wide", 1)], axis=0)

    (given, kept), late = root_solve(right, root_factor, leaf_mid)
    kept = total([kept, swap(given.astype(jnp.bfloat16), "wide", 1)])
    root_solution = relative_scatter(kept, "wide", 2)

    leaf_mid = hold(leaf_mid, late[-1])
    leaf_mid = lax.all_gather(leaf_mid, "narrow", axis=1, tiled=True).reshape(wide_count * rows, -1)

    wanted = landing.reshape(sect_count * wide_count, border_block, root_block)
    source = jnp.broadcast_to(root_solution[None], (sect_count * wide_count, rows, root_block))
    picked = lax.dot_general(
        source, wanted, (((2,), (2,)), ((0,), (0,))), preferred_element_type=jnp.float32
    )
    picked = lax.optimization_barrier(picked.astype(jnp.bfloat16))
    sent = hold(picked, leaf_mid).reshape(-1, small, border_block)
    got = lax.all_to_all(sent, ("sect", "wide", "narrow"), 0, 0, tiled=True)
    got = got.reshape(sect_count, wide_count, narrow_count, small, border_block)
    own = jnp.sum(got.astype(jnp.float32), axis=(0, 2)).astype(jnp.bfloat16)
    returned = direct_gather(by_relation(own), "narrow", 1).reshape(wide_count * rows, border_block)

    back_leaf = times(leaf_mid, leaf_factor) - times(returned, leaf_coupling)
    leaf_solution = relative_scatter(back_leaf, "wide")
    return (leaf_solution, root_solution)


def solution(mesh):
    in_specs = (
        P("wide", ("sect", "narrow")),
        P(("sect", "wide"), "narrow"),
        P(("sect", "wide"), "narrow"),
        P("wide", ("sect", "narrow")),
        P("wide", ("sect", "narrow")),
        P(),
        P(),
    )
    out_specs = (P("wide", ("sect", "narrow")), P("wide", ("sect", "narrow")))
    return jax.shard_map(body, mesh=mesh, in_specs=in_specs, out_specs=out_specs, check_vma=False)
```

```python
import jax
import jax.numpy as jnp
from jax import lax
from jax.sharding import PartitionSpec as P

CHUNKS = 4


def times_transposed(left, right):
    return lax.dot_general(
        left, right, (((1,), (1,)), ((), ())), preferred_element_type=jnp.float32
    )


def times(left, right):
    return jnp.dot(left, right, preferred_element_type=jnp.float32)


def hold(value, *others):
    corners = [lax.slice(o, (0,) * o.ndim, (1,) * o.ndim).reshape(()) for o in others]
    zero = lax.clamp(jnp.int32(0), sum(c.astype(jnp.int32) for c in corners), jnp.int32(0))
    return value + zero.astype(value.dtype)


def swap(value, axis, distance):
    pairs = [(i, i ^ distance) for i in range(lax.axis_size(axis))]
    return lax.ppermute(value, axis, pairs)


def total(values):
    result = values[0].astype(jnp.float32)
    for value in values[1:]:
        result = result + value.astype(jnp.float32)
    return result.astype(jnp.bfloat16)


def relative_gather(value, axis, last=1):
    distance = lax.axis_size(axis) // 2
    while distance >= last:
        value = jnp.concatenate([value, swap(value, axis, distance)], axis=0)
        distance //= 2
    return value


def relative_scatter(value, axis, distance=1):
    while distance < lax.axis_size(axis):
        half = value.shape[0] // 2
        value = total([value[:half], swap(value[half:].astype(jnp.bfloat16), axis, distance)])
        distance *= 2
    return value


def relative_places(axis):
    places = [0]
    distance = lax.axis_size(axis) // 2
    while distance >= 1:
        places = places + [place ^ distance for place in places]
        distance //= 2
    return places


def direct_scatter(value, axis, dim=0):
    count = lax.axis_size(axis)
    here = lax.axis_index(axis)
    block = value.shape[dim] // count
    shape = value.shape[:dim] + (count, block) + value.shape[dim + 1 :]
    blocks = value.reshape(shape)
    parts = [lax.dynamic_index_in_dim(blocks, here ^ k, dim, keepdims=False) for k in range(count)]
    return total([parts[0]] + [swap(parts[k], axis, k) for k in range(1, count)])


def direct_gather(value, axis, dim=0):
    count = lax.axis_size(axis)
    here = lax.axis_index(axis)
    shape = value.shape[:dim] + (count,) + value.shape[dim:]
    result = jnp.zeros(shape, value.dtype)
    for k in range(count):
        block = value if k == 0 else swap(value, axis, k)
        result = lax.dynamic_update_index_in_dim(result, block, here ^ k, dim)
    return result.reshape(value.shape[:dim] + (count * value.shape[dim],) + value.shape[dim + 1 :])


def halve(value, axis, distance, others=()):
    bit = (lax.axis_index(axis) // distance) % 2
    halves = value.reshape((2, value.shape[0] // 2) + value.shape[1:])
    kept, given = (lax.dynamic_index_in_dim(halves, k, 0, keepdims=False) for k in (bit, 1 - bit))
    if others:
        given = hold(given, *others)
    return total([kept, swap(given, axis, distance)])


def double(value, axis, distance):
    bit = (lax.axis_index(axis) // distance) % 2
    result = jnp.zeros((2,) + value.shape, value.dtype)
    result = lax.dynamic_update_index_in_dim(result, value, bit, 0)
    result = lax.dynamic_update_index_in_dim(result, swap(value, axis, distance), 1 - bit, 0)
    return result.reshape((2 * value.shape[0],) + value.shape[1:])


def distances(axis):
    return [(axis, 1 << k) for k in range(lax.axis_size(axis).bit_length() - 1)]


def sum_all(value, order, others):
    first = value = halve(value, *order[0], others)
    for axis, distance in order[1:]:
        value = halve(value, axis, distance)
    for axis, distance in reversed(order):
        value = double(value, axis, distance)
    return value, first


def root_solve(right, factor, beside):
    rows = factor.shape[0] // CHUNKS
    half = right.shape[0] // 2
    sect, narrow = distances("sect"), distances("narrow")
    orders = [sect + narrow, narrow[:1] + sect + narrow[1:]]
    blocks = [factor[c * rows : (c + 1) * rows] for c in range(CHUNKS)]
    middles, firsts = [], []
    for c in range(CHUNKS):
        product = times_transposed(right, blocks[c]).astype(jnp.bfloat16)
        others = [firsts[c - len(orders)]] if c >= len(orders) else ([beside] if c == 1 else [])
        middle, first = sum_all(product, orders[c % len(orders)], others)
        middles.append(middle)
        firsts.append(first)
    backs = []
    for part in (slice(half, None), slice(0, half)):
        back = None
        for c in range(CHUNKS):
            term = times(middles[c][part], blocks[c])
            back = term if back is None else back + term
        backs.append(back)
    return backs, middles


def body(leaf_rhs, leaf_factor, leaf_coupling, root_factor, root_rhs, border_map, border_rows):
    wide_count = lax.axis_size("wide")
    narrow_count = lax.axis_size("narrow")
    sect_count = lax.axis_size("sect")
    sect_index = lax.axis_index("sect")
    wide_index = lax.axis_index("wide")
    narrow_index = lax.axis_index("narrow")
    border_block = leaf_coupling.shape[0]
    border_total = border_block * wide_count
    rows = leaf_rhs.shape[0]
    small = rows // narrow_count
    root_block = root_rhs.shape[1]
    root_start = (sect_index * narrow_count + narrow_index) * root_block

    columns = lax.broadcasted_iota(jnp.int32, (1, 1, root_block), 2) + root_start
    border_place = lax.broadcasted_iota(jnp.int32, border_map.shape, 1)
    live_map = jnp.where(border_place < border_rows[:, None], border_map, -1)
    near_map = jnp.stack(
        [lax.dynamic_index_in_dim(live_map, sect_index ^ r, 0, keepdims=False) for r in range(sect_count)]
    )
    landing = (near_map[:, :, None] == columns).astype(jnp.bfloat16)

    piece = relative_gather(leaf_rhs, "wide")
    places = relative_places("wide")
    border_terms = times_transposed(piece, leaf_coupling).astype(jnp.bfloat16)
    blocks = border_terms.reshape(wide_count, rows, border_block)
    order = [places.index(k) for k in range(wide_count)]

    def by_place(values, dim=0):
        near = [lax.index_in_dim(values, order[k], dim, keepdims=False) for k in range(wide_count)]
        near = jnp.stack(near, axis=dim)
        return jnp.stack(
            [lax.dynamic_index_in_dim(near, wide_index ^ k, dim, keepdims=False) for k in range(wide_count)],
            axis=dim,
        )

    def by_relation(values, dim=0):
        return jnp.stack(
            [lax.dynamic_index_in_dim(values, wide_index ^ p, dim, keepdims=False) for p in places],
            axis=dim,
        )

    sent = by_place(blocks).reshape(wide_count * narrow_count, small, border_block)
    got = lax.all_to_all(sent, ("wide", "narrow"), 0, 0, tiled=True)
    border_sum = jnp.sum(
        got.reshape(wide_count, narrow_count, small, border_block).astype(jnp.float32), axis=1
    )
    border_out = border_sum.transpose(1, 0, 2).reshape(small, border_total).astype(jnp.bfloat16)

    updates = direct_gather(hold(border_out, landing), "narrow")
    pivot_terms = times_transposed(piece, leaf_factor).astype(jnp.bfloat16)
    pivot_terms = pivot_terms.reshape(wide_count, rows, -1)
    passed = hold(updates, pivot_terms)
    leaf_mid = lax.psum_scatter(pivot_terms, "narrow", scatter_dimension=1, tiled=True)
    others = [swap(passed, "sect", r) for r in range(1, sect_count)]
    landed = times(jnp.concatenate([updates] + others, axis=1), landing.reshape(-1, root_block))
    root_right = (root_rhs.astype(jnp.float32) - landed).astype(jnp.bfloat16)
    right = relative_gather(root_right, "wide", 2)
    right = jnp.concatenate([right, swap(right, "wide", 1)], axis=0)

    (given, kept), late = root_solve(right, root_factor, leaf_mid)
    given = swap(given.astype(jnp.bfloat16), "wide", 1)
    leaf_mid = hold(leaf_mid, given)
    kept = total([kept, given])
    root_solution = relative_scatter(kept, "wide", 2)

    leaf_mid = lax.all_gather(leaf_mid, "narrow", axis=1, tiled=True).reshape(wide_count * rows, -1)

    source = jnp.broadcast_to(root_solution[None], (wide_count, rows, root_block))
    picked = []
    for r in reversed(range(sect_count)):
        wanted = landing[r].reshape(wide_count, border_block, root_block)
        part = lax.dot_general(
            source, wanted, (((2,), (2,)), ((0,), (0,))), preferred_element_type=jnp.float32
        ).astype(jnp.bfloat16)
        part = lax.optimization_barrier(part)
        picked.append(swap(part, "sect", r) if r else part)
    sent = hold(total(picked), leaf_mid).reshape(-1, small, border_block)
    got = lax.all_to_all(sent, ("wide", "narrow"), 0, 0, tiled=True)
    got = got.reshape(wide_count, narrow_count, small, border_block)
    own = jnp.sum(got.astype(jnp.float32), axis=1).astype(jnp.bfloat16)
    returned = direct_gather(by_relation(own), "narrow", 1).reshape(wide_count * rows, border_block)

    back_leaf = times(leaf_mid, leaf_factor) - times(returned, leaf_coupling)
    leaf_solution = relative_scatter(back_leaf, "wide")
    return (leaf_solution, root_solution)


def solution(mesh):
    in_specs = (
        P("wide", ("sect", "narrow")),
        P(("sect", "wide"), "narrow"),
        P(("sect", "wide"), "narrow"),
        P("wide", ("sect", "narrow")),
        P("wide", ("sect", "narrow")),
        P(),
        P(),
    )
    out_specs = (P("wide", ("sect", "narrow")), P("wide", ("sect", "narrow")))
    return jax.shard_map(body, mesh=mesh, in_specs=in_specs, out_specs=out_specs, check_vma=False)
```

```python
import jax
import jax.numpy as jnp
from jax import lax
from jax.sharding import PartitionSpec as P

CHUNKS = 4


def times_transposed(left, right):
    return lax.dot_general(
        left, right, (((1,), (1,)), ((), ())), preferred_element_type=jnp.float32
    )


def times(left, right):
    return jnp.dot(left, right, preferred_element_type=jnp.float32)


def hold(value, *others):
    corners = [lax.slice(o, (0,) * o.ndim, (1,) * o.ndim).reshape(()) for o in others]
    zero = lax.clamp(jnp.int32(0), sum(c.astype(jnp.int32) for c in corners), jnp.int32(0))
    return value + zero.astype(value.dtype)


def swap(value, axis, distance):
    pairs = [(i, i ^ distance) for i in range(lax.axis_size(axis))]
    return lax.ppermute(value, axis, pairs)


def total(values):
    result = values[0].astype(jnp.float32)
    for value in values[1:]:
        result = result + value.astype(jnp.float32)
    return result.astype(jnp.bfloat16)


def relative_gather(value, axis, last=1):
    distance = lax.axis_size(axis) // 2
    while distance >= last:
        value = jnp.concatenate([value, swap(value, axis, distance)], axis=0)
        distance //= 2
    return value


def relative_scatter(value, axis, distance=1):
    while distance < lax.axis_size(axis):
        half = value.shape[0] // 2
        value = total([value[:half], swap(value[half:].astype(jnp.bfloat16), axis, distance)])
        distance *= 2
    return value


def relative_places(axis):
    places = [0]
    distance = lax.axis_size(axis) // 2
    while distance >= 1:
        places = places + [place ^ distance for place in places]
        distance //= 2
    return places


def direct_scatter(value, axis, dim=0):
    count = lax.axis_size(axis)
    here = lax.axis_index(axis)
    block = value.shape[dim] // count
    shape = value.shape[:dim] + (count, block) + value.shape[dim + 1 :]
    blocks = value.reshape(shape)
    parts = [lax.dynamic_index_in_dim(blocks, here ^ k, dim, keepdims=False) for k in range(count)]
    return total([parts[0]] + [swap(parts[k], axis, k) for k in range(1, count)])


def direct_gather(value, axis, dim=0):
    count = lax.axis_size(axis)
    here = lax.axis_index(axis)
    shape = value.shape[:dim] + (count,) + value.shape[dim:]
    result = jnp.zeros(shape, value.dtype)
    for k in range(count):
        block = value if k == 0 else swap(value, axis, k)
        result = lax.dynamic_update_index_in_dim(result, block, here ^ k, dim)
    return result.reshape(value.shape[:dim] + (count * value.shape[dim],) + value.shape[dim + 1 :])


def halve(value, axis, distance, others=()):
    bit = (lax.axis_index(axis) // distance) % 2
    halves = value.reshape((2, value.shape[0] // 2) + value.shape[1:])
    kept, given = (lax.dynamic_index_in_dim(halves, k, 0, keepdims=False) for k in (bit, 1 - bit))
    if others:
        given = hold(given, *others)
    return total([kept, swap(given, axis, distance)])


def double(value, axis, distance):
    bit = (lax.axis_index(axis) // distance) % 2
    result = jnp.zeros((2,) + value.shape, value.dtype)
    result = lax.dynamic_update_index_in_dim(result, value, bit, 0)
    result = lax.dynamic_update_index_in_dim(result, swap(value, axis, distance), 1 - bit, 0)
    return result.reshape((2 * value.shape[0],) + value.shape[1:])


def distances(axis):
    return [(axis, 1 << k) for k in range(lax.axis_size(axis).bit_length() - 1)]


def sum_all(value, order, others):
    first = value = halve(value, *order[0], others)
    for axis, distance in order[1:]:
        value = halve(value, axis, distance)
    for axis, distance in reversed(order):
        value = double(value, axis, distance)
    return value, first


def root_solve(right, factor, beside):
    rows = factor.shape[0] // CHUNKS
    half = right.shape[0] // 2
    sect, narrow = distances("sect"), distances("narrow")
    orders = [sect + narrow, narrow[:1] + sect + narrow[1:]]
    blocks = [factor[c * rows : (c + 1) * rows] for c in range(CHUNKS)]
    middles, firsts = [], []
    for c in range(CHUNKS):
        product = times_transposed(right, blocks[c]).astype(jnp.bfloat16)
        others = [firsts[c - len(orders)]] if c >= len(orders) else ([beside] if c == 0 else [])
        middle, first = sum_all(product, orders[c % len(orders)], others)
        middles.append(middle)
        firsts.append(first)
    backs = []
    for part in (slice(half, None), slice(0, half)):
        back = None
        for c in range(CHUNKS):
            term = times(middles[c][part], blocks[c])
            back = term if back is None else back + term
        backs.append(back)
    return backs, middles


def body(leaf_rhs, leaf_factor, leaf_coupling, root_factor, root_rhs, border_map, border_rows):
    wide_count = lax.axis_size("wide")
    narrow_count = lax.axis_size("narrow")
    sect_count = lax.axis_size("sect")
    sect_index = lax.axis_index("sect")
    wide_index = lax.axis_index("wide")
    narrow_index = lax.axis_index("narrow")
    border_block = leaf_coupling.shape[0]
    border_total = border_block * wide_count
    rows = leaf_rhs.shape[0]
    small = rows // narrow_count
    root_block = root_rhs.shape[1]
    root_start = (sect_index * narrow_count + narrow_index) * root_block

    columns = lax.broadcasted_iota(jnp.int32, (1, 1, root_block), 2) + root_start
    border_place = lax.broadcasted_iota(jnp.int32, border_map.shape, 1)
    live_map = jnp.where(border_place < border_rows[:, None], border_map, -1)
    near_map = jnp.stack(
        [lax.dynamic_index_in_dim(live_map, sect_index ^ r, 0, keepdims=False) for r in range(sect_count)]
    )
    landing = (near_map[:, :, None] == columns).astype(jnp.bfloat16)

    piece = relative_gather(leaf_rhs, "wide")
    places = relative_places("wide")
    border_terms = times_transposed(piece, leaf_coupling).astype(jnp.bfloat16)
    blocks = border_terms.reshape(wide_count, rows, border_block)
    order = [places.index(k) for k in range(wide_count)]

    def by_place(values, dim=0):
        near = [lax.index_in_dim(values, order[k], dim, keepdims=False) for k in range(wide_count)]
        near = jnp.stack(near, axis=dim)
        return jnp.stack(
            [lax.dynamic_index_in_dim(near, wide_index ^ k, dim, keepdims=False) for k in range(wide_count)],
            axis=dim,
        )

    def by_relation(values, dim=0):
        return jnp.stack(
            [lax.dynamic_index_in_dim(values, wide_index ^ p, dim, keepdims=False) for p in places],
            axis=dim,
        )

    sent = by_place(blocks).reshape(wide_count * narrow_count, small, border_block)
    got = lax.all_to_all(sent, ("wide", "narrow"), 0, 0, tiled=True)
    border_sum = jnp.sum(
        got.reshape(wide_count, narrow_count, small, border_block).astype(jnp.float32), axis=1
    )
    border_out = border_sum.transpose(1, 0, 2).reshape(small, border_total).astype(jnp.bfloat16)

    updates = direct_gather(hold(border_out, landing), "narrow")
    pivot_terms = times_transposed(piece, leaf_factor).astype(jnp.bfloat16)
    pivot_terms = lax.optimization_barrier(pivot_terms.reshape(wide_count, rows, -1))
    passed = hold(updates, pivot_terms)
    pivot_terms = hold(pivot_terms, updates)
    leaf_mid = lax.psum_scatter(pivot_terms, "narrow", scatter_dimension=1, tiled=True)
    landed = lax.optimization_barrier(times(updates, landing[0]))
    for r in range(1, sect_count):
        landed = landed + times(swap(passed, "sect", r), landing[r])
    root_right = (root_rhs.astype(jnp.float32) - landed).astype(jnp.bfloat16)
    right = relative_gather(root_right, "wide", 2)
    right = jnp.concatenate([right, swap(right, "wide", 1)], axis=0)

    (given, kept), late = root_solve(right, root_factor, leaf_mid)
    given = swap(given.astype(jnp.bfloat16), "wide", 1)
    leaf_mid = hold(leaf_mid, given)
    kept = total([kept, given])
    root_solution = relative_scatter(kept, "wide", 2)

    leaf_mid = lax.all_gather(leaf_mid, "narrow", axis=1, tiled=True).reshape(wide_count * rows, -1)

    source = jnp.broadcast_to(root_solution[None], (wide_count, rows, root_block))
    picked = []
    for r in reversed(range(sect_count)):
        wanted = landing[r].reshape(wide_count, border_block, root_block)
        part = lax.dot_general(
            source, wanted, (((2,), (2,)), ((0,), (0,))), preferred_element_type=jnp.float32
        ).astype(jnp.bfloat16)
        part = lax.optimization_barrier(part)
        picked.append(swap(part, "sect", r) if r else part)
    sent = hold(total(picked), leaf_mid).reshape(-1, small, border_block)
    got = lax.all_to_all(sent, ("wide", "narrow"), 0, 0, tiled=True)
    got = got.reshape(wide_count, narrow_count, small, border_block)
    own = jnp.sum(got.astype(jnp.float32), axis=1).astype(jnp.bfloat16)
    returned = direct_gather(by_relation(own), "narrow", 1).reshape(wide_count * rows, border_block)

    back_leaf = times(leaf_mid, leaf_factor) - times(returned, leaf_coupling)
    leaf_solution = relative_scatter(back_leaf, "wide")
    return (leaf_solution, root_solution)


def solution(mesh):
    in_specs = (
        P("wide", ("sect", "narrow")),
        P(("sect", "wide"), "narrow"),
        P(("sect", "wide"), "narrow"),
        P("wide", ("sect", "narrow")),
        P("wide", ("sect", "narrow")),
        P(),
        P(),
    )
    out_specs = (P("wide", ("sect", "narrow")), P("wide", ("sect", "narrow")))
    return jax.shard_map(body, mesh=mesh, in_specs=in_specs, out_specs=out_specs, check_vma=False)
```

```python
import jax
import jax.numpy as jnp
from jax import lax
from jax.sharding import PartitionSpec as P

CHUNKS = 4


def times_transposed(left, right):
    return lax.dot_general(
        left, right, (((1,), (1,)), ((), ())), preferred_element_type=jnp.float32
    )


def times(left, right):
    return jnp.dot(left, right, preferred_element_type=jnp.float32)


def hold(value, *others):
    corners = [lax.slice(o, (0,) * o.ndim, (1,) * o.ndim).reshape(()) for o in others]
    zero = lax.clamp(jnp.int32(0), sum(c.astype(jnp.int32) for c in corners), jnp.int32(0))
    return value + zero.astype(value.dtype)


def swap(value, axis, distance):
    pairs = [(i, i ^ distance) for i in range(lax.axis_size(axis))]
    return lax.ppermute(value, axis, pairs)


def total(values):
    result = values[0].astype(jnp.float32)
    for value in values[1:]:
        result = result + value.astype(jnp.float32)
    return result.astype(jnp.bfloat16)


def relative_gather(value, axis, last=1):
    distance = lax.axis_size(axis) // 2
    while distance >= last:
        value = jnp.concatenate([value, swap(value, axis, distance)], axis=0)
        distance //= 2
    return value


def relative_scatter(value, axis, distance=1):
    while distance < lax.axis_size(axis):
        half = value.shape[0] // 2
        value = total([value[:half], swap(value[half:].astype(jnp.bfloat16), axis, distance)])
        distance *= 2
    return value


def relative_places(axis):
    places = [0]
    distance = lax.axis_size(axis) // 2
    while distance >= 1:
        places = places + [place ^ distance for place in places]
        distance //= 2
    return places


def direct_scatter(value, axis, dim=0):
    count = lax.axis_size(axis)
    here = lax.axis_index(axis)
    block = value.shape[dim] // count
    shape = value.shape[:dim] + (count, block) + value.shape[dim + 1 :]
    blocks = value.reshape(shape)
    parts = [lax.dynamic_index_in_dim(blocks, here ^ k, dim, keepdims=False) for k in range(count)]
    return total([parts[0]] + [swap(parts[k], axis, k) for k in range(1, count)])


def direct_gather(value, axis, dim=0):
    count = lax.axis_size(axis)
    here = lax.axis_index(axis)
    shape = value.shape[:dim] + (count,) + value.shape[dim:]
    result = jnp.zeros(shape, value.dtype)
    for k in range(count):
        block = value if k == 0 else swap(value, axis, k)
        result = lax.dynamic_update_index_in_dim(result, block, here ^ k, dim)
    return result.reshape(value.shape[:dim] + (count * value.shape[dim],) + value.shape[dim + 1 :])


def halve(value, axis, distance, others=()):
    bit = (lax.axis_index(axis) // distance) % 2
    halves = value.reshape((2, value.shape[0] // 2) + value.shape[1:])
    kept, given = (lax.dynamic_index_in_dim(halves, k, 0, keepdims=False) for k in (bit, 1 - bit))
    if others:
        given = hold(given, *others)
    return total([kept, swap(given, axis, distance)])


def double(value, axis, distance):
    bit = (lax.axis_index(axis) // distance) % 2
    result = jnp.zeros((2,) + value.shape, value.dtype)
    result = lax.dynamic_update_index_in_dim(result, value, bit, 0)
    result = lax.dynamic_update_index_in_dim(result, swap(value, axis, distance), 1 - bit, 0)
    return result.reshape((2 * value.shape[0],) + value.shape[1:])


def distances(axis):
    return [(axis, 1 << k) for k in range(lax.axis_size(axis).bit_length() - 1)]


def sum_all(value, order, others):
    first = value = halve(value, *order[0], others)
    for axis, distance in order[1:]:
        value = halve(value, axis, distance)
    for axis, distance in reversed(order):
        value = double(value, axis, distance)
    return value, first


def root_solve(right, factor, beside):
    rows = factor.shape[0] // CHUNKS
    half = right.shape[0] // 2
    sect, narrow = distances("sect"), distances("narrow")
    orders = [sect + narrow, narrow[:1] + sect + narrow[1:]]
    blocks = [factor[c * rows : (c + 1) * rows] for c in range(CHUNKS)]
    middles, firsts = [], []
    for c in range(CHUNKS):
        product = times_transposed(right, blocks[c]).astype(jnp.bfloat16)
        others = [firsts[c - len(orders)]] if c >= len(orders) else ([beside] if c == 0 else [])
        middle, first = sum_all(product, orders[c % len(orders)], others)
        middles.append(middle)
        firsts.append(first)
    backs = []
    for part in (slice(half, None), slice(0, half)):
        back = None
        for c in range(CHUNKS):
            term = times(middles[c][part], blocks[c])
            back = term if back is None else back + term
        backs.append(back)
    return backs, middles


def body(leaf_rhs, leaf_factor, leaf_coupling, root_factor, root_rhs, border_map, border_rows):
    wide_count = lax.axis_size("wide")
    narrow_count = lax.axis_size("narrow")
    sect_count = lax.axis_size("sect")
    sect_index = lax.axis_index("sect")
    wide_index = lax.axis_index("wide")
    narrow_index = lax.axis_index("narrow")
    border_block = leaf_coupling.shape[0]
    border_total = border_block * wide_count
    rows = leaf_rhs.shape[0]
    small = rows // narrow_count
    root_block = root_rhs.shape[1]
    root_start = (sect_index * narrow_count + narrow_index) * root_block

    columns = lax.broadcasted_iota(jnp.int32, (1, 1, root_block), 2) + root_start
    border_place = lax.broadcasted_iota(jnp.int32, border_map.shape, 1)
    live_map = jnp.where(border_place < border_rows[:, None], border_map, -1)
    near_map = jnp.stack(
        [lax.dynamic_index_in_dim(live_map, sect_index ^ r, 0, keepdims=False) for r in range(sect_count)]
    )
    landing = (near_map[:, :, None] == columns).astype(jnp.bfloat16)

    piece = relative_gather(leaf_rhs, "wide")
    places = relative_places("wide")
    border_terms = times_transposed(piece, leaf_coupling).astype(jnp.bfloat16)
    blocks = border_terms.reshape(wide_count, rows, border_block)
    order = [places.index(k) for k in range(wide_count)]

    def by_place(values, dim=0):
        near = [lax.index_in_dim(values, order[k], dim, keepdims=False) for k in range(wide_count)]
        near = jnp.stack(near, axis=dim)
        return jnp.stack(
            [lax.dynamic_index_in_dim(near, wide_index ^ k, dim, keepdims=False) for k in range(wide_count)],
            axis=dim,
        )

    def by_relation(values, dim=0):
        return jnp.stack(
            [lax.dynamic_index_in_dim(values, wide_index ^ p, dim, keepdims=False) for p in places],
            axis=dim,
        )

    sent = by_place(blocks).reshape(wide_count * narrow_count, small, border_block)
    got = lax.all_to_all(sent, ("wide", "narrow"), 0, 0, tiled=True)
    border_sum = jnp.sum(
        got.reshape(wide_count, narrow_count, small, border_block).astype(jnp.float32), axis=1
    )
    border_out = border_sum.transpose(1, 0, 2).reshape(small, border_total).astype(jnp.bfloat16)

    updates = direct_gather(hold(border_out, landing), "narrow")
    pivot_terms = times_transposed(piece, leaf_factor).astype(jnp.bfloat16)
    pivot_terms = lax.optimization_barrier(pivot_terms.reshape(wide_count, rows, -1))
    passed = hold(updates, pivot_terms)
    pivot_terms = hold(pivot_terms, updates)
    leaf_mid = lax.psum_scatter(pivot_terms, "narrow", scatter_dimension=1, tiled=True)
    landed = lax.optimization_barrier(times(updates, landing[0]))
    for r in range(1, sect_count):
        landed = landed + times(swap(passed, "sect", r), landing[r])
    root_right = (root_rhs.astype(jnp.float32) - landed).astype(jnp.bfloat16)
    right = relative_gather(root_right, "wide", 2)
    right = jnp.concatenate([right, swap(right, "wide", 1)], axis=0)

    (given, kept), late = root_solve(right, root_factor, leaf_mid)
    given = swap(given.astype(jnp.bfloat16), "wide", 1)
    leaf_mid = hold(leaf_mid, given)
    kept = total([kept, given])
    root_solution = relative_scatter(kept, "wide", 2)

    leaf_mid = lax.all_gather(leaf_mid, "narrow", axis=1, tiled=True).reshape(wide_count * rows, -1)

    source = jnp.broadcast_to(root_solution[None], (wide_count, rows, root_block))
    picked = []
    for r in reversed(range(sect_count)):
        wanted = landing[r].reshape(wide_count, border_block, root_block)
        part = lax.dot_general(
            source, wanted, (((2,), (2,)), ((0,), (0,))), preferred_element_type=jnp.float32
        ).astype(jnp.bfloat16)
        part = lax.optimization_barrier(part)
        picked.append(swap(part, "sect", r) if r else part)
    sent = hold(total(picked), leaf_mid).reshape(-1, small, border_block)
    got = lax.all_to_all(sent, ("wide", "narrow"), 0, 0, tiled=True)
    got = got.reshape(wide_count, narrow_count, small, border_block)
    own = jnp.sum(got.astype(jnp.float32), axis=1).astype(jnp.bfloat16)
    own = by_relation(own)
    pieces = [swap(own, "narrow", k) if k else own for k in range(narrow_count)]
    middles = leaf_mid.reshape(wide_count, narrow_count, small, -1)
    leaf_solution = jnp.zeros((narrow_count, small, leaf_factor.shape[1]), jnp.bfloat16)
    group = max(1, narrow_count // 2)
    for first in range(0, narrow_count, group):
        near = range(first, first + group)
        returned = jnp.concatenate([pieces[k] for k in near], axis=1)
        middle = jnp.concatenate(
            [lax.dynamic_index_in_dim(middles, narrow_index ^ k, 1, keepdims=False) for k in near], axis=1
        )
        height = wide_count * group * small
        back_leaf = times(middle.reshape(height, -1), leaf_factor) - times(
            returned.reshape(height, -1), leaf_coupling
        )
        part = relative_scatter(back_leaf, "wide").reshape(group, small, -1)
        for k in near:
            leaf_solution = lax.dynamic_update_index_in_dim(leaf_solution, part[k - first], narrow_index ^ k, 0)
    leaf_solution = leaf_solution.reshape(rows, -1)
    return (leaf_solution, root_solution)


def solution(mesh):
    in_specs = (
        P("wide", ("sect", "narrow")),
        P(("sect", "wide"), "narrow"),
        P(("sect", "wide"), "narrow"),
        P("wide", ("sect", "narrow")),
        P("wide", ("sect", "narrow")),
        P(),
        P(),
    )
    out_specs = (P("wide", ("sect", "narrow")), P("wide", ("sect", "narrow")))
    return jax.shard_map(body, mesh=mesh, in_specs=in_specs, out_specs=out_specs, check_vma=False)
```

```python
import jax
import jax.numpy as jnp
from jax import lax
from jax.sharding import PartitionSpec as P

CHUNKS = 4


def times_transposed(left, right):
    return lax.dot_general(
        left, right, (((1,), (1,)), ((), ())), preferred_element_type=jnp.float32
    )


def times(left, right):
    return jnp.dot(left, right, preferred_element_type=jnp.float32)


def hold(value, *others):
    corners = [lax.slice(o, (0,) * o.ndim, (1,) * o.ndim).reshape(()) for o in others]
    zero = lax.clamp(jnp.int32(0), sum(c.astype(jnp.int32) for c in corners), jnp.int32(0))
    return value + zero.astype(value.dtype)


def swap(value, axis, distance):
    pairs = [(i, i ^ distance) for i in range(lax.axis_size(axis))]
    return lax.ppermute(value, axis, pairs)


def total(values):
    result = values[0].astype(jnp.float32)
    for value in values[1:]:
        result = result + value.astype(jnp.float32)
    return result.astype(jnp.bfloat16)


def relative_gather(value, axis, last=1):
    distance = lax.axis_size(axis) // 2
    while distance >= last:
        value = jnp.concatenate([value, swap(value, axis, distance)], axis=0)
        distance //= 2
    return value


def relative_scatter(low, high, axis):
    first = got = swap(high.astype(jnp.bfloat16), axis, 1)
    distance = 2
    while distance < lax.axis_size(axis):
        half = low.shape[0] // 2
        low, high = total([low[:half], got[:half]]), total([low[half:], got[half:]])
        got = swap(high, axis, distance)
        distance *= 2
    return total([low, got]), first


def relative_places(axis):
    places = [0]
    distance = lax.axis_size(axis) // 2
    while distance >= 1:
        places = places + [place ^ distance for place in places]
        distance //= 2
    return places


def direct_scatter(value, axis, dim=0):
    count = lax.axis_size(axis)
    here = lax.axis_index(axis)
    block = value.shape[dim] // count
    shape = value.shape[:dim] + (count, block) + value.shape[dim + 1 :]
    blocks = value.reshape(shape)
    parts = [lax.dynamic_index_in_dim(blocks, here ^ k, dim, keepdims=False) for k in range(count)]
    return total([parts[0]] + [swap(parts[k], axis, k) for k in range(1, count)])


def direct_gather(value, axis, dim=0):
    count = lax.axis_size(axis)
    here = lax.axis_index(axis)
    shape = value.shape[:dim] + (count,) + value.shape[dim:]
    result = jnp.zeros(shape, value.dtype)
    for k in range(count):
        block = value if k == 0 else swap(value, axis, k)
        result = lax.dynamic_update_index_in_dim(result, block, here ^ k, dim)
    return result.reshape(value.shape[:dim] + (count * value.shape[dim],) + value.shape[dim + 1 :])


def halve(value, axis, distance, others=()):
    bit = (lax.axis_index(axis) // distance) % 2
    halves = value.reshape((2, value.shape[0] // 2) + value.shape[1:])
    kept, given = (lax.dynamic_index_in_dim(halves, k, 0, keepdims=False) for k in (bit, 1 - bit))
    if others:
        given = hold(given, *others)
    return total([kept, swap(given, axis, distance)])


def double(value, axis, distance):
    bit = (lax.axis_index(axis) // distance) % 2
    result = jnp.zeros((2,) + value.shape, value.dtype)
    result = lax.dynamic_update_index_in_dim(result, value, bit, 0)
    result = lax.dynamic_update_index_in_dim(result, swap(value, axis, distance), 1 - bit, 0)
    return result.reshape((2 * value.shape[0],) + value.shape[1:])


def distances(axis):
    return [(axis, 1 << k) for k in range(lax.axis_size(axis).bit_length() - 1)]


def sum_all(value, order, others):
    first = value = halve(value, *order[0], others)
    for axis, distance in order[1:]:
        value = halve(value, axis, distance)
    for axis, distance in reversed(order):
        value = double(value, axis, distance)
    return value, first


def root_solve(right, factor, beside):
    rows = factor.shape[0] // CHUNKS
    half = right.shape[0] // 2
    sect, narrow = distances("sect"), distances("narrow")
    orders = [sect + narrow, narrow[:1] + sect + narrow[1:]]
    blocks = [factor[c * rows : (c + 1) * rows] for c in range(CHUNKS)]
    middles, firsts = [], []
    for c in range(CHUNKS):
        product = times_transposed(right, blocks[c]).astype(jnp.bfloat16)
        others = [firsts[c - len(orders)]] if c >= len(orders) else ([beside] if c == 0 else [])
        middle, first = sum_all(product, orders[c % len(orders)], others)
        middles.append(middle)
        firsts.append(first)
    backs = []
    for part in (slice(half, None), slice(0, half)):
        back = None
        for c in range(CHUNKS):
            term = times(middles[c][part], blocks[c])
            back = term if back is None else back + term
        backs.append(back)
    return backs, middles


def body(leaf_rhs, leaf_factor, leaf_coupling, root_factor, root_rhs, border_map, border_rows):
    wide_count = lax.axis_size("wide")
    narrow_count = lax.axis_size("narrow")
    sect_count = lax.axis_size("sect")
    sect_index = lax.axis_index("sect")
    wide_index = lax.axis_index("wide")
    narrow_index = lax.axis_index("narrow")
    border_block = leaf_coupling.shape[0]
    border_total = border_block * wide_count
    rows = leaf_rhs.shape[0]
    small = rows // narrow_count
    root_block = root_rhs.shape[1]
    root_start = (sect_index * narrow_count + narrow_index) * root_block

    columns = lax.broadcasted_iota(jnp.int32, (1, 1, root_block), 2) + root_start
    border_place = lax.broadcasted_iota(jnp.int32, border_map.shape, 1)
    live_map = jnp.where(border_place < border_rows[:, None], border_map, -1)
    near_map = jnp.stack(
        [lax.dynamic_index_in_dim(live_map, sect_index ^ r, 0, keepdims=False) for r in range(sect_count)]
    )
    landing = (near_map[:, :, None] == columns).astype(jnp.bfloat16)

    piece = relative_gather(leaf_rhs, "wide")
    places = relative_places("wide")
    border_terms = times_transposed(piece, leaf_coupling).astype(jnp.bfloat16)
    blocks = border_terms.reshape(wide_count, rows, border_block)
    order = [places.index(k) for k in range(wide_count)]

    def by_place(values, dim=0):
        near = [lax.index_in_dim(values, order[k], dim, keepdims=False) for k in range(wide_count)]
        near = jnp.stack(near, axis=dim)
        return jnp.stack(
            [lax.dynamic_index_in_dim(near, wide_index ^ k, dim, keepdims=False) for k in range(wide_count)],
            axis=dim,
        )

    def by_relation(values, dim=0):
        return jnp.stack(
            [lax.dynamic_index_in_dim(values, wide_index ^ p, dim, keepdims=False) for p in places],
            axis=dim,
        )

    sent = by_place(blocks).reshape(wide_count * narrow_count, small, border_block)
    got = lax.all_to_all(sent, ("wide", "narrow"), 0, 0, tiled=True)
    border_sum = jnp.sum(
        got.reshape(wide_count, narrow_count, small, border_block).astype(jnp.float32), axis=1
    )
    border_out = border_sum.transpose(1, 0, 2).reshape(small, border_total).astype(jnp.bfloat16)

    updates = direct_gather(hold(border_out, landing), "narrow")
    pivot_terms = times_transposed(piece, leaf_factor).astype(jnp.bfloat16)
    pivot_terms = lax.optimization_barrier(pivot_terms.reshape(wide_count, rows, -1))
    passed = hold(updates, pivot_terms)
    pivot_terms = hold(pivot_terms, updates)
    leaf_mid = lax.psum_scatter(pivot_terms, "narrow", scatter_dimension=1, tiled=True)
    landed = lax.optimization_barrier(times(updates, landing[0]))
    for r in range(1, sect_count):
        landed = landed + times(swap(passed, "sect", r), landing[r])
    root_right = (root_rhs.astype(jnp.float32) - landed).astype(jnp.bfloat16)
    right = relative_gather(root_right, "wide", 2)
    right = jnp.concatenate([right, swap(right, "wide", 1)], axis=0)

    (given, kept), late = root_solve(right, root_factor, leaf_mid)
    root_solution, brought = relative_scatter(kept, given, "wide")
    leaf_mid = hold(leaf_mid, brought)

    leaf_mid = lax.all_gather(leaf_mid, "narrow", axis=1, tiled=True).reshape(wide_count * rows, -1)

    source = jnp.broadcast_to(root_solution[None], (wide_count, rows, root_block))
    picked = []
    for r in reversed(range(sect_count)):
        wanted = landing[r].reshape(wide_count, border_block, root_block)
        part = lax.dot_general(
            source, wanted, (((2,), (2,)), ((0,), (0,))), preferred_element_type=jnp.float32
        ).astype(jnp.bfloat16)
        part = lax.optimization_barrier(part)
        picked.append(swap(part, "sect", r) if r else part)
    sent = hold(total(picked), leaf_mid).reshape(-1, small, border_block)
    got = lax.all_to_all(sent, ("wide", "narrow"), 0, 0, tiled=True)
    got = got.reshape(wide_count, narrow_count, small, border_block)
    own = jnp.sum(got.astype(jnp.float32), axis=1).astype(jnp.bfloat16)
    own = by_relation(own)
    pieces = [swap(own, "narrow", k) if k else own for k in range(narrow_count)]
    middles = leaf_mid.reshape(wide_count, narrow_count, small, -1)
    leaf_solution = jnp.zeros((narrow_count, small, leaf_factor.shape[1]), jnp.bfloat16)
    group = max(1, narrow_count // 2)
    for first in range(0, narrow_count, group):
        near = range(first, first + group)
        returned = jnp.concatenate([pieces[k] for k in near], axis=1)
        middle = jnp.concatenate(
            [lax.dynamic_index_in_dim(middles, narrow_index ^ k, 1, keepdims=False) for k in near], axis=1
        )
        height = wide_count * group * small
        back_leaf = times(middle.reshape(height, -1), leaf_factor) - times(
            returned.reshape(height, -1), leaf_coupling
        )
        part, _ = relative_scatter(back_leaf[: height // 2], back_leaf[height // 2 :], "wide")
        part = part.reshape(group, small, -1)
        for k in near:
            leaf_solution = lax.dynamic_update_index_in_dim(leaf_solution, part[k - first], narrow_index ^ k, 0)
    leaf_solution = leaf_solution.reshape(rows, -1)
    return (leaf_solution, root_solution)


def solution(mesh):
    in_specs = (
        P("wide", ("sect", "narrow")),
        P(("sect", "wide"), "narrow"),
        P(("sect", "wide"), "narrow"),
        P("wide", ("sect", "narrow")),
        P("wide", ("sect", "narrow")),
        P(),
        P(),
    )
    out_specs = (P("wide", ("sect", "narrow")), P("wide", ("sect", "narrow")))
    return jax.shard_map(body, mesh=mesh, in_specs=in_specs, out_specs=out_specs, check_vma=False)
```
